256 devices in a mesh: chol: 64 (over z, y_lo, x), walk: 4 (over y_hi, core).
Axes of the slice: x: 4, y: 4 (y_hi: 2, y_lo: 2; y = y_hi * 2 + y_lo), z: 8, core: 2. Of those that a mesh axis runs over, the one named last changes fastest.
Arguments:
- chol_full: float32 [768, 160000], P('chol'), may hold values from -0.109375 to 0.109375
- chol_half: bfloat16 [768, 24000], P('chol'), may hold values from -0.001953125 to 0.001953125
- walkers: bfloat16 [96, 24000], P('walk', 'chol'), may hold values from -6 to 6
- inv_intersection: bfloat16 [96, 60, 60], P('walk'), may hold values from -0.75 to 0.75
- fields: float32 [96, 768], P('walk', 'chol'), may hold values from -6 to 6
- log_weight: float32 [96], P('walk'), may hold values from -4 to 4
Outputs:
- new_walkers: bfloat16 [96, 24000], P('walk', 'chol')
- new_log_weight: float32 [96], P('walk')
- hartree: float32 [96], P('walk')
- mixed_energy: float32 [], replicated
The draws below stay inside these ranges and needn't reach their ends.
All inputs are finite; a program needn't handle non-finite values.
Results may differ from the reference program's by a relative error of at most 0.0034.
Values may be sent and summed in bfloat16 or wider, within the bound.
A program may use at most 128 MiB of HBM per device.

```python
import jax
import jax.numpy as jnp
from jax import lax

N = 400
NE = 60
ORDER = 3
NCHOL = 768
WALKERS = 96


def level_of(key, dims, cuts, smallest, high):
    def one(axis_at, shards_of):
        draws = jax.random.uniform(jax.random.fold_in(jax.random.fold_in(key, 6), axis_at), (shards_of,), jnp.float32, smallest / len(cuts), high / len(cuts))
        return jnp.repeat(jnp.exp(draws), dims[axis_at] // shards_of).reshape((-1,) + (1,) * (len(dims) - axis_at - 1))

    factor_of = one(*cuts[0])
    for cut in cuts[1:]:
        factor_of = factor_of * one(*cut)
    return factor_of


def scatter_about(key, shape, width, reach, pieces=(), dtype=jnp.bfloat16):
    gain = level_of(key, shape, pieces, -0.22, 0.18) if pieces else 1.0
    result = jax.random.normal(key, shape, jnp.float32) * width * gain
    return jnp.minimum(jnp.maximum(result, -reach), reach).astype(dtype)


def setup_inputs(seed: int = 0) -> dict:
    key_list = jax.random.split(jax.random.key(seed), 7)
    return {
        "chol_full": scatter_about(key_list[0], (NCHOL, N * N), (N * NCHOL // 100) ** -0.5, 0.109375, ((0, 64),), jnp.float32),
        "chol_half": scatter_about(key_list[1], (NCHOL, NE * N), (400 * N * NE) ** -0.5, 0.001953125, ((0, 64),)),
        "walkers": scatter_about(key_list[2], (WALKERS, NE * N), 1.0, 6.0, ((0, 4), (1, 64))),
        "inv_intersection": scatter_about(key_list[3], (WALKERS, NE, NE), NE ** -0.5, 0.75, ((0, 4),)),
        "fields": scatter_about(key_list[4], (WALKERS, NCHOL), 1.0, 6.0, ((0, 4), (1, 64)), jnp.float32),
        "log_weight": scatter_about(key_list[5], (WALKERS,), 1.0, 4.0, ((0, 4),), jnp.float32),
    }


field_step = 0.1
bias_coef = 2.0
bias_cap = 0.3


def reference(chol_full, chol_half, walkers, inv_intersection, fields, log_weight):
    count = walkers.shape[0]
    orbitals = walkers.reshape(count, NE, N)
    green = jnp.einsum('wba,wbi->wai', inv_intersection.astype(jnp.float32), orbitals.astype(jnp.float32)).astype(jnp.bfloat16)
    force_bias = jnp.dot(green.reshape(count, NE * N), chol_half.T, preferred_element_type=jnp.float32)
    bias_shift = jnp.clip(-bias_coef * force_bias, -bias_cap, bias_cap)
    field = fields - bias_shift
    increment = jnp.sum(fields * bias_shift - 0.5 * bias_shift * bias_shift, axis=1)
    hartree = 0.5 * jnp.sum(force_bias * force_bias, axis=1)
    operator = field_step * jnp.dot(field, chol_full, precision=lax.Precision.HIGHEST, preferred_element_type=jnp.float32)
    operator = operator.reshape(count, N, N)
    current = orbitals
    total = orbitals.astype(jnp.float32)
    for order in range(1, ORDER + 1):
        following = jnp.einsum('waj,wij->wai', current.astype(jnp.float32), operator, precision=lax.Precision.HIGHEST) / order
        total = total + following
        current = following.astype(jnp.bfloat16)
    new_walkers = total.reshape(count, NE * N).astype(jnp.bfloat16)
    new_log_weight = log_weight + increment
    weights = jnp.exp(new_log_weight)
    mixed_energy = jnp.sum(weights * hartree) / jnp.sum(weights)
    return (new_walkers, new_log_weight, hartree, mixed_energy)
```

```python
import jax
import jax.numpy as jnp
from jax import lax
from jax.experimental import pallas as pl
from jax.experimental.pallas import tpu as pltpu
from jax.sharding import PartitionSpec as P

N = 400
NE = 60
ORDER = 3
GROUP = 24
SHARDS = 64
VECTORS = 12
PIECE = 375
COLS = 640
BLOCKS = 250
PLANE = 8
DEPTH = 8
SLICE = 24
LANE = 128
EARLY = 28
STRIDE = 27

field_step = 0.1
bias_coef = 2.0
bias_cap = 0.3

f32 = jnp.float32
bf16 = jnp.bfloat16


def first_tile(r):
    return (N * r) // LANE


def wait_bytes(ref, sem):
    pltpu.make_async_copy(ref, ref, sem).wait()


def kernel(
    chol_hbm, half_hbm, walkers_hbm, inv_hbm, fields_hbm, logw_hbm,
    out_ref, newlog_ref, hartree_ref, mixed_ref,
    half_ref, walkers_ref, inv_ref, fields_ref, logw_ref, cin, csend, crecv, psrc, pp,
    tiles3, tiles4, orb, gflat, gsend, grecv, gf, hsend, hrecv, fsend, frecv,
    f1send, f1recv, f2all, opbuf, oprecv, abuf, xbuf, termt, total, nsend, nrecv,
    in_sem, c_send, c_recv, p_send, p_recv, g_send, g_recv, h_send, h_recv, f_send, f_recv,
    f1_send, f1_recv, f2_send, f2_recv, f3_send, f3_recv, o_send, o_recv, n_send, n_recv,
):
    c = lax.axis_index("chol")
    wk = lax.axis_index("walk")
    core = wk % 2
    z = c // PLANE
    p = c % PLANE
    block = wk * SHARDS + c
    mine = 3 * z + p // 2
    owns = jnp.logical_and((p + core) % 2 == 0, p < 6)
    place = pl.multiple_of(wk * GROUP, 8)

    def owner_of(walker, group):
        return PLANE * (walker // 3) + 2 * (walker % 3) + group % 2

    def send(src, dst, s_sem, r_sem, chol, walk):
        pltpu.make_async_remote_copy(
            src_ref=src, dst_ref=dst, send_sem=s_sem, recv_sem=r_sem,
            device_id={"chol": chol, "walk": walk}, device_id_type=pl.DeviceIdType.MESH,
        ).start()

    base = wk * (SHARDS * COLS) - (wk // 3) * 3840
    pairs = (
        (walkers_hbm, walkers_ref),
        (fields_hbm, fields_ref),
        (half_hbm, half_ref),
        (chol_hbm.at[:, pl.ds(pl.multiple_of(base, LANE), SHARDS * COLS)], cin),
        (inv_hbm, inv_ref),
        (logw_hbm, logw_ref),
    )
    copies = [pltpu.make_async_copy(src, dst, in_sem.at[i]) for i, (src, dst) in enumerate(pairs)]
    for copy in copies:
        copy.start()

    barrier = pltpu.get_barrier_semaphore()

    def greet(i, _):
        pl.semaphore_signal(
            barrier, inc=1, device_id={"chol": (c + i) % SHARDS, "walk": wk},
            device_id_type=pl.DeviceIdType.MESH,
        )
        return 0

    lax.fori_loop(1, SHARDS, greet, 0)
    other_core = wk + 1 - 2 * core
    other_half = (wk + 2) % 4
    beside = PLANE * z + (p + 4) % PLANE
    third = (other_core + 2) % 4
    for chol, walk in ((c, other_core), (beside, other_half), (beside, third)):
        pl.semaphore_signal(
            barrier, inc=1, device_id={"chol": chol, "walk": walk}, device_id_type=pl.DeviceIdType.MESH
        )

    copies[0].wait()
    psrc[...] = jnp.concatenate(
        [walkers_ref[...].astype(f32), jnp.zeros((GROUP, 384 - PIECE), f32)], axis=1
    )
    copies[1].wait()
    fields = jnp.concatenate([fields_ref[...], jnp.zeros((4, GROUP), f32)], axis=0).T
    fields = jnp.concatenate([fields, jnp.zeros((GROUP, 112), f32)], axis=1)
    fsend[...] = pltpu.roll(fields, 16 * p, 1)
    frecv[p] = fsend[...]
    pl.semaphore_wait(barrier, SHARDS + 2)

    def send_piece(i, _):
        walker = (i + c) % GROUP
        owner = owner_of(walker, wk)

        @pl.when(owner != c)
        def _():
            send(psrc.at[pl.ds(walker, 1)], pp.at[pl.ds(c, 1)], p_send, p_recv, owner, wk)

        @pl.when(owner == c)
        def _():
            pltpu.make_async_copy(psrc.at[pl.ds(walker, 1)], pp.at[pl.ds(c, 1)], p_recv).start()

        return 0

    lax.fori_loop(0, GROUP, send_piece, 0)

    copies[4].wait()
    copies[5].wait()

    @pl.when(owns)
    def _():
        third = lax.broadcasted_iota(jnp.int32, (NE, GROUP, NE), 1)
        inverse = jnp.sum(jnp.where(third == mine, inv_ref[...].astype(f32), 0.0), axis=1)
        inverse = jnp.concatenate([inverse, jnp.zeros((4, NE), f32)], axis=0)
        inverse = jnp.concatenate([inverse, jnp.zeros((64, 4), f32)], axis=1).T.astype(bf16)
        wait_bytes(pp, p_recv)
        for q in range(3):
            tiles3[q] = pp[:, q * LANE : (q + 1) * LANE]
        for q in range(4):
            tiles4[q] = jnp.zeros((64, LANE), f32)
        rows = [
            jnp.concatenate([tiles3[q, pl.ds(s, 4, stride=16), :] for q in range(3)], axis=1)
            for s in range(16)
        ]
        for b in range(15):
            line = jnp.concatenate(
                [rows[b][:, 25 * b : PIECE], rows[b + 1][:, : 25 * (b + 1)], jnp.zeros((4, 112), f32)],
                axis=1,
            )
            for q in range(4):
                tiles4[q, pl.ds(b, 4, stride=15), :] = line[:, q * LANE : (q + 1) * LANE]
        orbitals = jnp.concatenate([tiles4[q] for q in range(4)], axis=1)
        green = jnp.dot(inverse, orbitals.astype(bf16), preferred_element_type=f32)
        for q in range(4):
            tiles4[q] = green[:, q * LANE : (q + 1) * LANE]
        flat = [jnp.zeros((8, LANE), f32) for _ in range(25)]
        for r in range(8):
            line = jnp.concatenate([tiles4[q, pl.ds(r, 8, stride=8), :] for q in range(4)], axis=1)
            if r:
                line = pltpu.roll(line, 16 * r, 1)
            for q in range(4):
                flat[first_tile(r) + q] = flat[first_tile(r) + q] + line[:, q * LANE : (q + 1) * LANE]
        for t in range(25):
            gflat[pl.ds(t, 8, stride=25), :] = flat[t]
        for q in range(PLANE):
            part = gflat[SLICE * q : SLICE * (q + 1), :]
            gsend[q] = jnp.concatenate([part, jnp.zeros((8, LANE), f32)], axis=0).astype(bf16)
        grecv[mine] = gsend[p]

        def spread(k, _):
            d = (c + STRIDE * k) % SHARDS
            send(gsend.at[d % PLANE], grecv.at[mine], g_send, g_recv.at[z], d, wk)
            return 0

        lax.fori_loop(1, SHARDS, spread, 0)
        orb[...] = orbitals

    copies[2].wait()
    for q in range(PLANE):
        width = min(SLICE * LANE, NE * N - q * SLICE * LANE)
        part = half_ref[:, q * SLICE * LANE : q * SLICE * LANE + width].astype(f32)
        if width < SLICE * LANE:
            part = jnp.concatenate([part, jnp.zeros((VECTORS, SLICE * LANE - width), f32)], axis=1)
        part = jnp.concatenate([part, jnp.zeros((4, SLICE * LANE), f32)], axis=0)
        hsend[q] = part.astype(bf16)
    row = pl.multiple_of(p * 16, 16)
    hrecv[pl.ds(row, 16), :] = hsend[p]

    def to_plane(k, _):
        q = (p + k) % PLANE
        send(hsend.at[q], hrecv.at[pl.ds(row, 16)], h_send, h_recv, PLANE * z + q, wk)
        send(fsend, frecv.at[p], f_send, f_recv, PLANE * z + q, wk)
        return 0

    lax.fori_loop(1, PLANE, to_plane, 0)

    def cut(d):
        at = (wk // 3) * 3840 + d * COLS - (wk // 3) * (d // 58) * (d - 57) * COLS
        part = cin[:, pl.ds(pl.multiple_of(at, LANE), COLS)]
        last = part[:, 512:]
        under = jnp.concatenate([last[0:4], last[4:8], last[8:12], jnp.zeros((4, LANE), f32)], axis=1)
        return jnp.concatenate([part[:, :512], under], axis=0).astype(bf16)

    slot = pl.multiple_of(c * 16, 16)

    def send_columns(i, _):
        d = (c + STRIDE * i) % SHARDS
        csend[d] = cut(d)
        send(csend.at[d], crecv.at[pl.ds(slot, 16)], c_send, c_recv, d, wk)
        return 0

    copies[3].wait()
    lax.fori_loop(1, EARLY, send_columns, 0)
    @pl.when(owns)
    def _():
        wait_bytes(grecv.at[pl.ds(0, 2)], g_recv.at[z])

    @pl.when(jnp.logical_not(owns))
    def _():
        wait_bytes(grecv.at[pl.ds(0, 3)], g_recv.at[z])

    lax.fori_loop(EARLY, SHARDS, send_columns, 0)
    crecv[pl.ds(slot, 16), :] = cut(c)

    def rest(k, _):
        wait_bytes(grecv.at[pl.ds(0, 3)], g_recv.at[(z + k) % DEPTH])
        return 0

    lax.fori_loop(1, DEPTH, rest, 0)

    for w in range(GROUP):
        gf[32 * w : 32 * w + 32, :] = grecv[w].astype(f32)
    green = jnp.concatenate(
        [gf[pl.ds(t, GROUP, stride=32), :] for t in range(SLICE)], axis=1
    ).astype(bf16)
    wait_bytes(gf.at[pl.ds(0, 7 * GROUP)], f_recv)
    wait_bytes(hrecv.at[pl.ds(0, 7 * 16)], h_recv)
    f1send[...] = lax.dot_general(
        green, hrecv[...], (((1,), (1,)), ((), ())), preferred_element_type=f32
    )
    f1recv[p] = f1send[...]

    def partial_bias(k, _):
        send(f1send, f1recv.at[p], f1_send, f1_recv, PLANE * z + (p + k) % PLANE, wk)
        return 0

    lax.fori_loop(1, PLANE, partial_bias, 0)
    wait_bytes(gf.at[pl.ds(0, 7 * GROUP)], f1_recv)
    force_bias = f1recv[0]
    fields = frecv[0]
    for q in range(1, PLANE):
        force_bias = force_bias + f1recv[q]
        fields = fields + frecv[q]
    shift = jnp.clip(-bias_coef * force_bias, -bias_cap, bias_cap)
    plane_log = jnp.sum(fields * shift - 0.5 * shift * shift, axis=1, keepdims=True)
    plane_energy = 0.5 * jnp.sum(force_bias * force_bias, axis=1, keepdims=True)
    eye = (
        lax.broadcasted_iota(jnp.int32, (GROUP, GROUP), 0)
        == lax.broadcasted_iota(jnp.int32, (GROUP, GROUP), 1)
    )
    log_column = jnp.sum(jnp.where(eye, logw_ref[...], 0.0), axis=1, keepdims=True)
    lane = lax.broadcasted_iota(jnp.int32, (GROUP, LANE), 1)
    wide = fields - shift
    wide = jnp.where(lane == 12, plane_log, wide)
    wide = jnp.where(lane == 13, plane_energy, wide)
    wide = jnp.where(lane == 14, log_column, wide)

    f2all[z, pl.ds(place, GROUP), :] = wide
    planes = f2all.at[z, pl.ds(place, GROUP)]

    def fields_z(k, _):
        send(planes, planes, f2_send, f2_recv, c + PLANE * ((z + k) % DEPTH - z), wk)
        return 0

    lax.fori_loop(1, DEPTH, fields_z, 0)
    wait_bytes(gf.at[pl.ds(0, 7 * GROUP)], f2_recv)
    own = f2all.at[:, pl.ds(place, GROUP)]

    def part(group, k):
        return f2all.at[k, pl.ds(pl.multiple_of(group * GROUP, 8), GROUP)]

    def to_half(k, _):
        send(part(wk, k), part(wk, k), f3_send.at[0], f3_recv.at[0], beside, other_half)
        return 0

    def to_core(k, _):
        send(part(wk, k), part(wk, k), f3_send.at[1], f3_recv.at[1], c, other_core)
        return 0

    def to_third(k, _):
        send(part(wk, k), part(wk, k), f3_send.at[2], f3_recv.at[2], beside, third)
        return 0

    lax.fori_loop(0, DEPTH, to_core, 0)
    lax.fori_loop(0, DEPTH, to_half, 0)
    lax.fori_loop(0, DEPTH, to_third, 0)
    wait_bytes(own, f3_recv.at[1])

    wait_bytes(crecv.at[pl.ds(0, 63 * 16)], c_recv)
    lane96 = lax.broadcasted_iota(jnp.int32, (96, LANE), 1)
    under48 = lane96[:48] % 16 >= 12

    def both(x):
        high = x.astype(bf16)
        return jnp.concatenate([high, (x - high.astype(f32)).astype(bf16)], axis=0)

    def blocks(pair):
        at = pl.multiple_of(48 * pair, 16)

        def block_step(b, acc):
            field = f2all[b, pl.ds(at, 48), :]
            rows = crecv[pl.ds(pl.multiple_of(b * LANE, LANE), LANE), :]
            upper = jnp.dot(both(jnp.where(under48, 0.0, field)), rows, preferred_element_type=f32)
            last = acc[1]
            for q in range(3):
                turned = jnp.where(under48, pltpu.roll(field, 12 - 4 * q, 1), 0.0)
                last = last + jnp.dot(
                    both(turned), rows[:, q * LANE : (q + 1) * LANE], preferred_element_type=f32
                )
            return acc[0] + upper, last

        acc, last = lax.fori_loop(
            0, DEPTH, block_step, (jnp.zeros((96, 512), f32), jnp.zeros((96, LANE), f32))
        )
        for t in range(5):
            part = acc[:, t * LANE : (t + 1) * LANE] if t < 4 else last
            opbuf[pl.ds(8 * at + t, 48, stride=8), :] = field_step * (part[:48] + part[48:])

        def send_block(i, _):
            w = at + (19 * i + block) % 48
            group = w // GROUP
            owner = owner_of(w % GROUP, group)
            me = jnp.logical_and(owner == c, group == wk)
            src = opbuf.at[pl.ds(pl.multiple_of(8 * w, 8), 5)]
            dst = oprecv.at[pl.ds(5 * block, 5)]

            @pl.when(jnp.logical_not(me))
            def _():
                send(src, dst, o_send, o_recv, owner, group)

            @pl.when(me)
            def _():
                pltpu.make_async_copy(src, dst, o_recv).start()

            return 0

        @pl.when(block < BLOCKS)
        def _():
            lax.fori_loop(0, 48, send_block, 0)

    blocks(wk // 2)
    wait_bytes(own, f3_recv.at[0])
    wait_bytes(own, f3_recv.at[2])
    blocks(1 - wk // 2)

    sums = f2all[0]
    for b in range(1, DEPTH):
        sums = sums + f2all[b]
    increment = jnp.sum(jnp.where(lane96 == 12, sums, 0.0), axis=1, keepdims=True)
    energy = jnp.sum(jnp.where(lane96 == 13, sums, 0.0), axis=1, keepdims=True)
    logs = jnp.sum(jnp.where(lane96 == 14, f2all[0], 0.0), axis=1, keepdims=True) + increment
    weight = jnp.exp(logs)
    mixed_ref[...] = jnp.sum(weight * energy, axis=0, keepdims=True) / jnp.sum(weight, axis=0, keepdims=True)
    own_log = jnp.zeros((GROUP, 1), f32)
    own_energy = jnp.zeros((GROUP, 1), f32)
    for g in range(4):
        own_log = jnp.where(wk == g, logs[g * GROUP : (g + 1) * GROUP], own_log)
        own_energy = jnp.where(wk == g, energy[g * GROUP : (g + 1) * GROUP], own_energy)
    newlog_ref[...] = jnp.sum(jnp.where(eye, own_log, 0.0), axis=0, keepdims=True)
    hartree_ref[...] = jnp.sum(jnp.where(eye, own_energy, 0.0), axis=0, keepdims=True)

    @pl.when(owns)
    def _():
        start = jnp.concatenate([orb[...].T[:N], jnp.zeros((N, 64), f32)], axis=1)
        total[...] = start
        xbuf[0:112, :] = jnp.zeros((112, LANE), bf16)
        xbuf[512:624, :] = jnp.zeros((112, LANE), bf16)
        xbuf[112:512, :] = start.astype(bf16)
        wait_bytes(oprecv, o_recv)
        for t in range(25):
            abuf[0:50, t * LANE : (t + 1) * LANE] = oprecv[pl.ds(t, 50, stride=25), :].astype(bf16)
        for k in range(1, ORDER + 1):
            for r in range(8):
                at = first_tile(r) * LANE
                value = jnp.dot(
                    abuf[0:50, at : at + 512], xbuf[112 - 16 * r : 624 - 16 * r, :],
                    preferred_element_type=f32,
                )
                termt[pl.ds(r, 50, stride=8), :] = value / k
            term = termt[...]
            total[...] += term
            if k < ORDER:
                xbuf[112:512, :] = term.astype(bf16)
        new = total[...].astype(bf16).astype(f32).T[:64]
        new = jnp.concatenate([new, jnp.zeros((64, 112), f32)], axis=1)
        for q in range(4):
            tiles4[q] = new[:, q * LANE : (q + 1) * LANE]
        rows = [
            jnp.concatenate([tiles4[q, pl.ds(b, 4, stride=15), :] for q in range(4)], axis=1)
            for b in range(15)
        ]
        for s in range(16):
            parts = []
            if s > 0:
                parts.append(rows[s - 1][:, N - 25 * s : N])
            if s < 15:
                parts.append(rows[s][:, : PIECE - 25 * s])
            piece = jnp.concatenate(parts + [jnp.zeros((4, 384 - PIECE), f32)], axis=1)
            for q in range(3):
                tiles3[q, pl.ds(s, 4, stride=16), :] = piece[:, q * LANE : (q + 1) * LANE]
        for q in range(3):
            nsend[:, q * LANE : (q + 1) * LANE] = tiles3[q]
        pltpu.make_async_copy(nsend.at[pl.ds(c, 1)], nrecv.at[pl.ds(mine, 1)], n_recv).start()

        def scatter(k, _):
            to = (c + STRIDE * k) % SHARDS
            send(nsend.at[pl.ds(to, 1)], nrecv.at[pl.ds(mine, 1)], n_send, n_recv, to, wk)
            return 0

        lax.fori_loop(1, SHARDS, scatter, 0)

    wait_bytes(nrecv, n_recv)
    out_ref[...] = nrecv[:, :PIECE].astype(bf16)

    wait_bytes(crecv.at[pl.ds(0, 63 * 16)], c_send)
    wait_bytes(hrecv.at[pl.ds(0, 7 * 16)], h_send)
    wait_bytes(gf.at[pl.ds(0, 7 * GROUP)], f_send)
    wait_bytes(gf.at[pl.ds(0, 7 * GROUP)], f1_send)
    wait_bytes(gf.at[pl.ds(0, 7 * GROUP)], f2_send)
    for k in range(3):
        wait_bytes(own, f3_send.at[k])

    @pl.when(owns)
    def _():
        wait_bytes(gf.at[pl.ds(0, 23 * 3)], p_send)
        wait_bytes(gf.at[pl.ds(0, 63 * 16)], g_send)
        wait_bytes(gf.at[pl.ds(0, 63 * 3)], n_send)

    @pl.when(jnp.logical_not(owns))
    def _():
        wait_bytes(gf.at[pl.ds(0, 24 * 3)], p_send)

    @pl.when(jnp.logical_and(block < BLOCKS, owns))
    def _():
        wait_bytes(opbuf.at[pl.ds(0, 475)], o_send)

    @pl.when(jnp.logical_and(block < BLOCKS, jnp.logical_not(owns)))
    def _():
        wait_bytes(opbuf.at[pl.ds(0, 480)], o_send)


def on_device(chol_full, chol_half, walkers, inv_intersection, fields, log_weight):
    vmem = pl.BlockSpec(memory_space=pltpu.VMEM)
    dma = pltpu.SemaphoreType.DMA
    new_walkers, new_log, hartree, mixed = pl.pallas_call(
        kernel,
        out_shape=(
            jax.ShapeDtypeStruct((GROUP, PIECE), bf16),
            jax.ShapeDtypeStruct((1, GROUP), f32),
            jax.ShapeDtypeStruct((1, GROUP), f32),
            jax.ShapeDtypeStruct((1, 1), f32),
        ),
        in_specs=[pl.BlockSpec(memory_space=pltpu.HBM)] * 6,
        out_specs=(vmem,) * 4,
        scratch_shapes=[
            pltpu.VMEM((VECTORS, NE * N), bf16),
            pltpu.VMEM((GROUP, PIECE), bf16),
            pltpu.VMEM((NE, GROUP, NE), bf16),
            pltpu.VMEM((VECTORS, GROUP), f32),
            pltpu.VMEM((1, GROUP), f32),
            pltpu.VMEM((VECTORS, SHARDS * COLS), f32),
            pltpu.VMEM((SHARDS, 16, 512), bf16),
            pltpu.VMEM((SHARDS * 16, 512), bf16),
            pltpu.VMEM((GROUP, 384), f32),
            pltpu.VMEM((SHARDS, 384), f32),
            pltpu.VMEM((3, 64, LANE), f32),
            pltpu.VMEM((4, 64, LANE), f32),
            pltpu.VMEM((64, 512), f32),
            pltpu.VMEM((200, LANE), f32),
            pltpu.VMEM((PLANE, 32, LANE), bf16),
            pltpu.VMEM((GROUP, 32, LANE), bf16),
            pltpu.VMEM((1024, LANE), f32),
            pltpu.VMEM((PLANE, 16, SLICE * LANE), bf16),
            pltpu.VMEM((PLANE * 16, SLICE * LANE), bf16),
            pltpu.VMEM((GROUP, LANE), f32),
            pltpu.VMEM((PLANE, GROUP, LANE), f32),
            pltpu.VMEM((GROUP, LANE), f32),
            pltpu.VMEM((PLANE, GROUP, LANE), f32),
            pltpu.VMEM((DEPTH, 96, LANE), f32),
            pltpu.VMEM((96 * 8, LANE), f32),
            pltpu.VMEM((BLOCKS * 5, LANE), f32),
            pltpu.VMEM((64, 25 * LANE), bf16),
            pltpu.VMEM((624, LANE), bf16),
            pltpu.VMEM((N, LANE), f32),
            pltpu.VMEM((N, LANE), f32),
            pltpu.VMEM((SHARDS, 384), f32),
            pltpu.VMEM((GROUP, 384), f32),
            dma((6,)),
        ] + [dma] * 5 + [dma((DEPTH,))] + [dma] * 8 + [dma((3,)), dma((3,))] + [dma] * 4,
        compiler_params=pltpu.CompilerParams(
            has_side_effects=True, collective_id=0, vmem_limit_bytes=60 * 1024 * 1024
        ),
        name="propagate",
    )(
        chol_full, chol_half, walkers, inv_intersection.transpose(1, 0, 2), fields.T,
        log_weight.reshape(1, GROUP),
    )
    return new_walkers, new_log.reshape(GROUP), hartree.reshape(GROUP), mixed.reshape(())


def solution(mesh):
    return jax.shard_map(
        on_device,
        mesh=mesh,
        in_specs=(
            P("chol", None),
            P("chol", None),
            P("walk", "chol"),
            P("walk", None, None),
            P("walk", "chol"),
            P("walk"),
        ),
        out_specs=(P("walk", "chol"), P("walk"), P("walk"), P()),
        check_vma=False,
    )
```
